512 devices in a mesh: shell: 64 (over x, y, z_lo), lat: 8 (over z_hi, core).
Axes of the slice: x: 4, y: 8, z: 8 (z_hi: 4, z_lo: 2; z = z_hi * 2 + z_lo), core: 2. Of those that a mesh axis runs over, the one named last changes fastest.
Arguments:
- advective_warming: bfloat16 [256, 768, 1536], P('shell', 'lat'), may hold values from -6 to 6
- associated_polynomial_table: bfloat16 [128, 768, 512], P(None, 'lat', 'shell'), may hold values from -12 to 12, as said below
- thermal_field: float32 [512, 128, 2, 256], P('shell', 'lat'), may hold values from -6 to 6
- operator_reciprocal: float32 [512, 256, 256], P('shell'), may hold values from -1 to 3, as said below
Outputs:
- new_temperature: float32 [512, 128, 2, 256], P('shell', 'lat')
The draws below stay inside these ranges and needn't reach their ends.
Inputs may be any that keep to these rules, and one draw needn't show every extreme that they name: `associated_polynomial_table`: zero wherever the degree l is below the order j * 4. `operator_reciprocal`: one matrix of order 256 for each degree.
All inputs are finite; a program needn't handle non-finite values.
Results may differ from the reference program's by a relative error of at most 0.007.
Values may be sent and summed in bfloat16 or wider, within the bound.
A program may use at most 128 MiB of HBM per device.

```python
import math
import jax
import jax.numpy as jnp
from jax import lax

NLAT = 768
NLON = 1536
LMAX_BOUND = 512
DEPTH_NODES = 256
AZIMUTH_MODES = 128


def draw_associated_polynomial_table(key, part):
    first = jax.random.fold_in(jax.random.fold_in(key, 11), 0)
    values = jnp.clip(jax.random.normal(first, (AZIMUTH_MODES, NLAT, LMAX_BOUND), jnp.float32), -6.0, 6.0) * 2.0
    degree = lax.broadcasted_iota(jnp.int32, (AZIMUTH_MODES, NLAT, LMAX_BOUND), 2)
    harmonic = lax.broadcasted_iota(jnp.int32, (AZIMUTH_MODES, NLAT, LMAX_BOUND), 0) * (LMAX_BOUND // AZIMUTH_MODES)
    return jnp.where(degree >= harmonic, values, 0.0).astype(jnp.bfloat16)


def draw_operator_reciprocal(key, part):
    first, second = jax.random.split(jax.random.fold_in(key, 23))
    spread = 0.3 / math.sqrt(DEPTH_NODES)
    coupling = jnp.clip(jax.random.normal(first, (LMAX_BOUND, DEPTH_NODES, DEPTH_NODES), jnp.float32), -3.0, 3.0) * spread
    diagonal = jax.random.uniform(second, (LMAX_BOUND, DEPTH_NODES, 1), jnp.float32, 1.0, 2.0)
    identity = jnp.eye(DEPTH_NODES, dtype=jnp.float32)
    return coupling + identity[None, :, :] * diagonal


def steps_of(own_key, extent, cuts, least, top_value):
    def one(dim, parts):
        draws = jax.random.uniform(jax.random.fold_in(jax.random.fold_in(own_key, 6), dim), (parts,), jnp.float32, least / len(cuts), top_value / len(cuts))
        return jnp.repeat(jnp.exp(draws), extent[dim] // parts).reshape((-1,) + (1,) * (len(extent) - dim - 1))

    level = one(*cuts[0])
    for cut in cuts[1:]:
        level = level * one(*cut)
    return level


def centred(key, extent, width, bound, cuts=(), kind=jnp.bfloat16):
    drawn = width * jax.random.normal(key, extent, jnp.float32)
    if cuts:
        drawn = drawn * steps_of(key, extent, cuts, -0.22, 0.18)
    return jnp.clip(drawn, -bound, bound).astype(kind)


def setup_inputs(seed: int = 0) -> dict:
    seeds = jax.random.split(jax.random.key(seed), 5)
    return {
        "advective_warming": centred(seeds[0], (DEPTH_NODES, NLAT, NLON), 1.0, 6.0, ((0, 64), (1, 8))),
        "associated_polynomial_table": draw_associated_polynomial_table(jax.random.fold_in(seeds[4], 71), 0),
        "thermal_field": centred(seeds[2], (LMAX_BOUND, AZIMUTH_MODES, 2, DEPTH_NODES), 1.0, 6.0, ((0, 64), (1, 8)), jnp.float32),
        "operator_reciprocal": draw_operator_reciprocal(jax.random.fold_in(seeds[4], 71), 0),
    }


def analysis_rows(orders, stride, longitudes):
    column = lax.broadcasted_iota(jnp.int32, (orders, longitudes), 1)
    harmonic = lax.broadcasted_iota(jnp.int32, (orders, longitudes), 0) * stride
    phased = (harmonic * column) % longitudes
    angles = phased.astype(jnp.float32) * (2.0 * math.pi / longitudes)
    stacked = jnp.stack([jnp.cos(angles), -jnp.sin(angles)], axis=1) / longitudes
    return stacked.reshape(2 * orders, longitudes).astype(jnp.bfloat16)


def reference(advective_warming, associated_polynomial_table, thermal_field, operator_reciprocal):
    analysis = analysis_rows(AZIMUTH_MODES, LMAX_BOUND // AZIMUTH_MODES, NLON)
    fourier = lax.dot_general(analysis, advective_warming.reshape(DEPTH_NODES * NLAT, NLON), (((1,), (1,)), ((), ())), preferred_element_type=jnp.float32)
    fourier = fourier.astype(jnp.bfloat16).reshape(AZIMUTH_MODES, 2, DEPTH_NODES, NLAT)
    surface_expansion = jnp.einsum("mcrt,mtl->mcrl", fourier.astype(jnp.float32), associated_polynomial_table.astype(jnp.float32), precision=lax.Precision.HIGHEST)
    warming_coefficients = thermal_field + 0.5 * jnp.transpose(surface_expansion, (3, 0, 1, 2))
    return jnp.einsum("lij,lmcj->lmci", operator_reciprocal, warming_coefficients, precision=lax.Precision.HIGHEST)
```

```python
import math

import jax
import jax.numpy as jnp
import numpy as np
from jax import lax
from jax.sharding import Mesh, PartitionSpec as P

backward_euler_update = 0.5


def analysis_rows(orders, stride, longitudes):
    phase = (np.arange(orders)[:, None] * stride * np.arange(longitudes)[None, :]) % longitudes
    angles = phase.astype(np.float32) * np.float32(2.0 * math.pi / longitudes)
    stacked = np.stack([np.cos(angles), -np.sin(angles)], axis=1) / np.float32(longitudes)
    return jnp.asarray(stacked.reshape(2 * orders, longitudes)).astype(jnp.bfloat16)


def shards(advective_warming, table, thermal_field, operator_reciprocal):
    radial_levels, bands, longitudes = advective_warming.shape
    orders = table.shape[0]
    own_degrees = table.shape[2]
    degrees = own_degrees * lax.axis_size("x") * lax.axis_size("g")
    table = lax.all_to_all(table, "lat", split_axis=0, concat_axis=1, tiled=True)
    table = lax.all_to_all(table, "g", split_axis=0, concat_axis=2, tiled=True)
    table = lax.all_gather(table, "x", axis=2, tiled=True)
    analysis = analysis_rows(orders, degrees // orders, longitudes)
    fourier = lax.dot_general(
        analysis,
        advective_warming.reshape(radial_levels * bands, longitudes),
        (((1,), (1,)), ((), ())),
        preferred_element_type=jnp.float32,
    )
    fourier = fourier.astype(jnp.bfloat16).reshape(orders, 2, radial_levels, bands)
    fourier = lax.all_to_all(fourier, "lat", split_axis=0, concat_axis=3, tiled=True)
    fourier = lax.all_to_all(fourier, "g", split_axis=0, concat_axis=2, tiled=True)
    block = jnp.einsum("mcrt,mtl->mcrl", fourier, table, preferred_element_type=jnp.float32)
    own_levels = block.shape[2]
    block = lax.all_to_all(
        block.astype(jnp.bfloat16), ("x", "g"), split_axis=3, concat_axis=0, tiled=True
    ).astype(jnp.float32)
    block = block.reshape(-1, thermal_field.shape[1], 2, own_levels, own_degrees)
    block = jnp.transpose(block, (4, 1, 2, 0, 3)).reshape(thermal_field.shape)
    forcing = thermal_field + backward_euler_update * block
    return jnp.einsum(
        "lij,lmcj->lmci", operator_reciprocal, forcing, precision=lax.Precision.HIGHEST
    )


def solution(mesh):
    shells, lats = mesh.devices.shape
    finer = Mesh(mesh.devices.reshape(4, shells // 4, lats), ("x", "g", "lat"))
    shell = ("x", "g")
    in_specs = (
        P(shell, "lat", None),
        P(None, "lat", shell),
        P(shell, "lat", None, None),
        P(shell, None, None),
    )
    out_specs = P(shell, "lat", None, None)
    return jax.shard_map(shards, mesh=finer, in_specs=in_specs, out_specs=out_specs, check_vma=False)
```

```python
import functools
import math

import jax
import jax.numpy as jnp
import numpy as np
from jax import lax
from jax.experimental import pallas as pl
from jax.experimental.pallas import tpu as pltpu
from jax.sharding import Mesh, PartitionSpec as P

backward_euler_update = 0.5
MESH = pl.DeviceIdType.MESH
NT = (((1,), (1,)), ((), ()))
f32, bf16 = jnp.float32, jnp.bfloat16


def analysis_rows(orders, stride, longitudes):
    phase = (np.arange(orders)[:, None] * stride * np.arange(longitudes)[None, :]) % longitudes
    angles = phase.astype(np.float32) * np.float32(2.0 * math.pi / longitudes)
    stacked = np.stack([np.cos(angles), -np.sin(angles)], axis=0) / np.float32(longitudes)
    return jnp.asarray(stacked.reshape(2 * orders, longitudes)).astype(bf16)


def level_order(xs, ks, own_levels):
    n = xs * ks * 2 * own_levels
    x, k, c, r = np.unravel_index(np.arange(n), (xs, ks, 2, own_levels))
    matrix = np.zeros((n, n), np.float32)
    matrix[np.arange(n), np.ravel_multi_index((c, x, k, r), (2, xs, ks, own_levels))] = backward_euler_update
    return jnp.asarray(matrix).astype(bf16)


def split(value):
    high = value.astype(bf16)
    return high, (value - high.astype(f32)).astype(bf16)


def kernel(
    sizes,
    warm_hbm, table_hbm, thermal_hbm, operator_hbm, analysis_hbm, order_hbm,
    out_ref,
    warm, table, thermal, operator, analysis, order,
    rows32, turned32, f_send, f_recv, p_send, p_all, s_send, s_recv, operator16, own_part, ordered32,
    load_sems, f_sems, p_sems, x_send_sems, x_recv_sems, s_sems,
):
    X, Y, A, B, C = sizes
    K = Y * A
    M = B * C * K
    x, y, a = lax.axis_index("x"), lax.axis_index("y"), lax.axis_index("a")
    b, c = lax.axis_index("b"), lax.axis_index("c")
    k = y * A + a
    me = (b * C + c) * K + k
    own_levels, bands, longitudes = warm.shape
    own_degrees = table.shape[1]
    lanes = f_send.shape[2]

    def owner(m):
        return {
            "b": m // (C * K), "c": lax.rem(m // K, C),
            "y": lax.rem(m, K) // A, "a": lax.rem(m, A),
        }

    def shell(s):
        return {"x": s // K, "y": lax.rem(s, K) // A, "a": lax.rem(s, A)}

    loads = [
        pltpu.make_async_copy(src, dst, load_sems.at[i])
        for i, (src, dst) in enumerate((
            (table_hbm, table), (warm_hbm, warm), (analysis_hbm, analysis),
            (thermal_hbm, thermal), (operator_hbm, operator), (order_hbm, order),
        ))
    ]
    for load in loads:
        load.start()

    barrier = pltpu.get_barrier_semaphore()

    def greet_plane(i, carry):
        pl.semaphore_signal(
            barrier, inc=1, device_id=owner(lax.rem(me + i, M)), device_id_type=MESH
        )
        return carry

    lax.fori_loop(1, M, greet_plane, 0)

    def greet_shell(i, carry):
        s = lax.rem(x * K + K + i, X * K)
        pl.semaphore_signal(barrier, inc=1, device_id=shell(s), device_id_type=MESH)
        return carry

    lax.fori_loop(0, (X - 1) * K, greet_shell, 0)

    loads[0].wait()
    rows32[...] = table[...].astype(f32).reshape(bands * own_degrees, M)
    for l in range(own_degrees):
        part = rows32[pl.ds(l, bands, stride=own_degrees), :]
        part = jnp.concatenate([part, jnp.zeros((lanes - bands, M), f32)], axis=0)
        turned32[pl.ds(l, M, stride=own_degrees), :] = part.T
    p_send[...] = turned32[...].reshape(M, own_degrees, lanes).astype(bf16)

    loads[1].wait()
    loads[2].wait()
    for r in range(own_levels):
        part = lax.dot_general(analysis[...], warm[r], NT, preferred_element_type=f32)
        part = jnp.concatenate([part, jnp.zeros((2 * M, lanes - bands), f32)], axis=1)
        for half in range(2):
            turned32[pl.ds(half * own_levels + r, M, stride=2 * own_levels), :] = part[
                half * M : (half + 1) * M
            ]
    f_send[...] = turned32[...].reshape(M, 2 * own_levels, lanes).astype(bf16)

    pl.semaphore_wait(barrier, M - 1 + (X - 1) * K)

    def p_copy(m):
        return pltpu.make_async_remote_copy(
            src_ref=p_send.at[m], dst_ref=p_all.at[x, me],
            send_sem=p_sems.at[0], recv_sem=p_sems.at[1],
            device_id=owner(m), device_id_type=MESH,
        )

    def f_copy(m):
        return pltpu.make_async_remote_copy(
            src_ref=f_send.at[m], dst_ref=f_recv.at[me],
            send_sem=f_sems.at[0], recv_sem=f_sems.at[1],
            device_id=owner(m), device_id_type=MESH,
        )

    def send_p(i, carry):
        p_copy(lax.rem(me + i, M)).start()
        return carry

    def send_f(i, carry):
        f_copy(lax.rem(me + i, M)).start()
        return carry

    pltpu.make_async_copy(p_send.at[me], p_all.at[x, me], p_sems.at[1]).start()
    lax.fori_loop(1, M, send_p, 0)
    pltpu.make_async_copy(f_send.at[me], f_recv.at[me], f_sems.at[1]).start()
    lax.fori_loop(1, M, send_f, 0)

    loads[3].wait()
    loads[4].wait()
    for l in range(own_degrees):
        high, low = split(operator[l])
        operator16[l] = high
        t_high, t_low = split(thermal[l])
        own_part[l] = (
            lax.dot_general(t_high, high, NT, preferred_element_type=f32)
            + lax.dot_general(t_low, high, NT, preferred_element_type=f32)
            + lax.dot_general(t_high, low, NT, preferred_element_type=f32)
        )
    loads[5].wait()

    pltpu.make_async_copy(p_all.at[x], p_all.at[x], p_sems.at[1]).wait()
    passed = []
    for d in range(1, X):
        copy = pltpu.make_async_remote_copy(
            src_ref=p_all.at[x], dst_ref=p_all.at[x],
            send_sem=x_send_sems.at[d - 1], recv_sem=x_recv_sems.at[d - 1],
            device_id={"x": lax.rem(x + d, X)}, device_id_type=MESH,
        )
        copy.start()
        passed.append(copy)
    for d in range(1, X):
        source = lax.rem(x - d + X, X)
        pltpu.make_async_copy(p_all.at[source], p_all.at[source], x_recv_sems.at[d - 1]).wait()
    pltpu.make_async_copy(f_recv, f_recv, f_sems.at[1]).wait()

    total = jnp.zeros((X * K * own_degrees, K * 2 * own_levels), f32)
    for band in range(B * C):
        here = pl.ds(band * K, K)
        total += lax.dot_general(
            p_all[:, here].reshape(X * K * own_degrees, lanes),
            f_recv[here].reshape(K * 2 * own_levels, lanes),
            NT, preferred_element_type=f32,
        )
    s_send[...] = total.reshape(X * K, own_degrees, K * 2 * own_levels).astype(bf16)

    me_shell = x * K + k

    def s_copy(s):
        return pltpu.make_async_remote_copy(
            src_ref=s_send.at[s], dst_ref=s_recv.at[x, k],
            send_sem=s_sems.at[0], recv_sem=s_sems.at[1],
            device_id=shell(s), device_id_type=MESH,
        )

    def send_s(i, carry):
        s_copy(lax.rem(me_shell + i, X * K)).start()
        return carry

    pltpu.make_async_copy(s_send.at[me_shell], s_recv.at[x, k], s_sems.at[1]).start()
    lax.fori_loop(1, X * K, send_s, 0)
    pltpu.make_async_copy(s_recv, s_recv, s_sems.at[1]).wait()

    width = K * 2 * own_levels
    half = X * K * own_levels
    ordered = jnp.zeros((K * own_degrees, 2 * half), f32)
    for xs in range(X):
        ordered += jnp.dot(
            s_recv[xs].reshape(K * own_degrees, width),
            order[xs * width : (xs + 1) * width],
            preferred_element_type=f32,
        )
    rows, wide = K * own_degrees, ordered32.shape[1]
    pieces = 2 * half // wide
    for piece in range(pieces):
        ordered32[piece * rows : (piece + 1) * rows] = ordered[:, piece * wide : (piece + 1) * wide]
    for l in range(own_degrees):
        parts = [
            ordered32[pl.ds(piece * rows + l, K, stride=own_degrees), :] for piece in range(pieces)
        ]
        forced = jnp.concatenate(
            [
                jnp.concatenate(parts[: pieces // 2], axis=1),
                jnp.concatenate(parts[pieces // 2 :], axis=1),
            ],
            axis=0,
        )
        out_ref[l] = own_part[l] + lax.dot_general(
            forced.astype(bf16), operator16[l], NT, preferred_element_type=f32
        )

    for copy in passed:
        copy.wait_send()
    for buffer, sems in ((p_send, p_sems), (f_send, f_sems), (s_send, s_sems)):
        sent = buffer.at[pl.ds(0, buffer.shape[0] - 1)]
        pltpu.make_async_copy(sent, sent, sems.at[0]).wait()


def shards(sizes, warming, table, thermal, operator):
    X, Y, A, B, C = sizes
    K = Y * A
    M = table.shape[0]
    own_levels, bands, longitudes = warming.shape
    own_degrees = table.shape[2]
    degrees = own_degrees * X * K
    levels = thermal.shape[3]
    lanes = 128
    vmem = pltpu.VMEM
    dma = pltpu.SemaphoreType.DMA
    table = jnp.transpose(table, (1, 2, 0))
    thermal = jnp.transpose(thermal, (0, 2, 1, 3)).reshape(own_degrees, 2 * K, levels)
    analysis = analysis_rows(M, degrees // M, longitudes)
    order = level_order(X, K, own_levels)
    result = pl.pallas_call(
        functools.partial(kernel, sizes),
        out_shape=jax.ShapeDtypeStruct((own_degrees, 2 * K, levels), f32),
        in_specs=[pl.BlockSpec(memory_space=pl.ANY)] * 6,
        out_specs=pl.BlockSpec(memory_space=pltpu.VMEM),
        scratch_shapes=[
            vmem(warming.shape, bf16),
            vmem(table.shape, bf16),
            vmem(thermal.shape, f32),
            vmem(operator.shape, f32),
            vmem(analysis.shape, bf16),
            vmem(order.shape, bf16),
            vmem((bands * own_degrees, M), f32),
            vmem((M * own_degrees, lanes), f32),
            vmem((M, 2 * own_levels, lanes), bf16),
            vmem((M, 2 * own_levels, lanes), bf16),
            vmem((M, own_degrees, lanes), bf16),
            vmem((X, M, own_degrees, lanes), bf16),
            vmem((X * K, own_degrees, K * 2 * own_levels), bf16),
            vmem((X, K, own_degrees, K * 2 * own_levels), bf16),
            vmem(operator.shape, bf16),
            vmem((own_degrees, 2 * K, levels), f32),
            vmem((2 * levels // min(lanes, levels) * K * own_degrees, min(lanes, levels)), f32),
            dma((6,)), dma((2,)), dma((2,)), dma((X - 1,)), dma((X - 1,)), dma((2,)),
        ],
        compiler_params=pltpu.CompilerParams(
            collective_id=0, has_side_effects=True, vmem_limit_bytes=40 * 2**20
        ),
        cost_estimate=pl.CostEstimate(flops=10**9, bytes_accessed=10**7, transcendentals=0),
    )(warming, table, thermal, operator, analysis, order)
    return jnp.transpose(result.reshape(own_degrees, 2, K, levels), (0, 2, 1, 3))


def build(mesh, sizes):
    finer = Mesh(mesh.devices.reshape(sizes), ("x", "y", "a", "b", "c"))
    shell, lat = ("x", "y", "a"), ("b", "c")
    in_specs = (
        P(shell, lat, None),
        P(None, lat, shell),
        P(shell, lat, None, None),
        P(shell, None, None),
    )
    return jax.shard_map(
        functools.partial(shards, sizes), mesh=finer, in_specs=in_specs,
        out_specs=P(shell, lat, None, None), check_vma=False,
    )


def solution(mesh):
    return build(mesh, (4, 8, 2, 4, 2))
```

```python
import functools
import math

import jax
import jax.numpy as jnp
import numpy as np
from jax import lax
from jax.experimental import pallas as pl
from jax.experimental.pallas import tpu as pltpu
from jax.sharding import Mesh, PartitionSpec as P

backward_euler_update = 0.5
MESH = pl.DeviceIdType.MESH
NT = (((1,), (1,)), ((), ()))
f32, bf16 = jnp.float32, jnp.bfloat16


def analysis_rows(orders, stride, longitudes):
    phase = (np.arange(orders)[:, None] * stride * np.arange(longitudes)[None, :]) % longitudes
    angles = phase.astype(np.float32) * np.float32(2.0 * math.pi / longitudes)
    stacked = np.stack([np.cos(angles), -np.sin(angles)], axis=0) / np.float32(longitudes)
    return jnp.asarray(stacked.reshape(2 * orders, longitudes)).astype(bf16)


def level_order(xs, ks, own_levels):
    n = xs * ks * 2 * own_levels
    x, k, c, r = np.unravel_index(np.arange(n), (xs, ks, 2, own_levels))
    matrix = np.zeros((n, n), np.float32)
    matrix[np.arange(n), np.ravel_multi_index((c, x, k, r), (2, xs, ks, own_levels))] = backward_euler_update
    return jnp.asarray(matrix).astype(bf16)


def split(value):
    high = value.astype(bf16)
    return high, (value - high.astype(f32)).astype(bf16)


def kernel(
    sizes,
    warm_hbm, table_hbm, thermal_hbm, operator_hbm, analysis_hbm, order_hbm,
    out_ref,
    warm, table, thermal, operator, analysis, order,
    rows32, turned32, f_send, f_recv, p_send, p_all, s_send, s_recv, operator16, own_part, ordered32,
    load_sems, f_sems, p_send_sem, p_sems, x_send_sems, x_recv_sems, s_sems, plane_sem,
):
    X, Y, A, B, C = sizes
    K = Y * A
    M = B * C * K
    x, y, a = lax.axis_index("x"), lax.axis_index("y"), lax.axis_index("a")
    b, c = lax.axis_index("b"), lax.axis_index("c")
    k = y * A + a
    me = (b * C + c) * K + k
    own_levels, bands, longitudes = warm.shape
    own_degrees = table.shape[1]
    lanes = f_send.shape[2]

    def owner(m):
        return {
            "b": m // (C * K), "c": lax.rem(m // K, C),
            "y": lax.rem(m, K) // A, "a": lax.rem(m, A),
        }

    def shell(s):
        return {"x": s // K, "y": lax.rem(s, K) // A, "a": lax.rem(s, A)}

    loads = [
        pltpu.make_async_copy(src, dst, load_sems.at[i])
        for i, (src, dst) in enumerate((
            (table_hbm, table), (warm_hbm, warm), (analysis_hbm, analysis),
            (thermal_hbm, thermal), (operator_hbm, operator), (order_hbm, order),
        ))
    ]
    for load in loads:
        load.start()

    barrier = pltpu.get_barrier_semaphore()

    def plane(dy, da, db, dc):
        return {
            "y": lax.rem(y + dy, Y), "a": lax.rem(a + da, A),
            "b": lax.rem(b + db, B), "c": lax.rem(c + dc, C),
        }

    columns = [(0, da, db, dc) for da in range(A) for db in range(B) for dc in range(C)][1:]
    rows = [(dy, 0, 0, 0) for dy in range(1, Y)]
    for step in columns + rows:
        pl.semaphore_signal(barrier, inc=1, device_id=plane(*step), device_id_type=MESH)
    for d in range(1, X):
        pl.semaphore_signal(
            barrier, inc=1, device_id={"x": lax.rem(x + d, X)}, device_id_type=MESH
        )

    loads[0].wait()
    rows32[...] = table[...].astype(f32).reshape(bands * own_degrees, M)
    for l in range(own_degrees):
        part = rows32[pl.ds(l, bands, stride=own_degrees), :]
        part = jnp.concatenate([part, jnp.zeros((lanes - bands, M), f32)], axis=0)
        turned32[pl.ds(l, M, stride=own_degrees), :] = part.T
    p_send[...] = turned32[...].reshape(M, own_degrees, lanes).astype(bf16)

    pl.semaphore_wait(barrier, len(columns) + len(rows) + X - 1)
    for step in rows:
        pl.semaphore_signal(plane_sem, inc=1, device_id=plane(*step), device_id_type=MESH)

    loads[1].wait()
    loads[2].wait()
    for r in range(own_levels):
        part = lax.dot_general(analysis[...], warm[r], NT, preferred_element_type=f32)
        part = jnp.concatenate([part, jnp.zeros((2 * M, lanes - bands), f32)], axis=1)
        for half in range(2):
            turned32[pl.ds(half * own_levels + r, M, stride=2 * own_levels), :] = part[
                half * M : (half + 1) * M
            ]
    f_send[...] = turned32[...].reshape(M, 2 * own_levels, lanes).astype(bf16)

    pl.semaphore_wait(plane_sem, len(rows))

    def p_copy(m, chunk):
        return pltpu.make_async_remote_copy(
            src_ref=p_send.at[m], dst_ref=p_all.at[x, me],
            send_sem=p_send_sem, recv_sem=p_sems.at[chunk],
            device_id=owner(m), device_id_type=MESH,
        )

    def f_copy(m, chunk):
        return pltpu.make_async_remote_copy(
            src_ref=f_send.at[m], dst_ref=f_recv.at[me],
            send_sem=f_sems.at[0], recv_sem=f_sems.at[1],
            device_id=owner(m), device_id_type=MESH,
        )

    chunks = sorted(
        ((db, dc) for db in range(B) for dc in range(C)),
        key=lambda step: -min(step[0], B - step[0]),
    )
    for copy in (p_copy, f_copy):
        for chunk, (db, dc) in enumerate(chunks):
            band = lax.rem(b + db, B) * C + lax.rem(c + dc, C)
            own = db == 0 and dc == 0

            def send(i, carry, copy=copy, chunk=chunk, band=band):
                copy(band * K + lax.rem(k + i, K), chunk).start()
                return carry

            lax.fori_loop(1 if own else 0, K, send, 0)
            if own and copy is p_copy:
                pltpu.make_async_copy(p_send.at[me], p_all.at[x, me], p_sems.at[chunk]).start()
            elif own:
                pltpu.make_async_copy(f_send.at[me], f_recv.at[me], f_sems.at[1]).start()

    loads[3].wait()
    loads[4].wait()
    for l in range(own_degrees):
        high, low = split(operator[l])
        operator16[l] = high
        t_high, t_low = split(
            jnp.concatenate([thermal[l, :, half, :] for half in range(2)], axis=0)
        )
        own_part[l] = (
            lax.dot_general(t_high, high, NT, preferred_element_type=f32)
            + lax.dot_general(t_low, high, NT, preferred_element_type=f32)
            + lax.dot_general(t_high, low, NT, preferred_element_type=f32)
        )
    loads[5].wait()

    for chunk, (db, dc) in enumerate(chunks):
        band = lax.rem(b - db + B, B) * C + lax.rem(c - dc + C, C)
        block = p_all.at[x, pl.ds(band * K, K)]
        pltpu.make_async_copy(block, block, p_sems.at[chunk]).wait()
        for d in range(1, X):
            copy = pltpu.make_async_remote_copy(
                src_ref=block, dst_ref=block,
                send_sem=x_send_sems.at[d - 1], recv_sem=x_recv_sems.at[d - 1],
                device_id={"x": lax.rem(x + d, X)}, device_id_type=MESH,
            )
            copy.start()
    for d in range(1, X):
        source = lax.rem(x - d + X, X)
        pltpu.make_async_copy(p_all.at[source], p_all.at[source], x_recv_sems.at[d - 1]).wait()
    pltpu.make_async_copy(f_recv, f_recv, f_sems.at[1]).wait()

    total = jnp.zeros((X * K * own_degrees, K * 2 * own_levels), f32)
    for band in range(B * C):
        here = pl.ds(band * K, K)
        total += lax.dot_general(
            p_all[:, here].reshape(X * K * own_degrees, lanes),
            f_recv[here].reshape(K * 2 * own_levels, lanes),
            NT, preferred_element_type=f32,
        )
    s_send[...] = total.reshape(X * K, own_degrees, K * 2 * own_levels).astype(bf16)

    me_shell = x * K + k

    def s_copy(s):
        return pltpu.make_async_remote_copy(
            src_ref=s_send.at[s], dst_ref=s_recv.at[x, k],
            send_sem=s_sems.at[0], recv_sem=s_sems.at[1],
            device_id=shell(s), device_id_type=MESH,
        )

    def send_s(i, carry):
        s_copy(lax.rem(me_shell + i, X * K)).start()
        return carry

    pltpu.make_async_copy(s_send.at[me_shell], s_recv.at[x, k], s_sems.at[1]).start()
    lax.fori_loop(1, X * K, send_s, 0)
    pltpu.make_async_copy(s_recv, s_recv, s_sems.at[1]).wait()

    width = K * 2 * own_levels
    half = X * K * own_levels
    ordered = jnp.zeros((K * own_degrees, 2 * half), f32)
    for xs in range(X):
        ordered += jnp.dot(
            s_recv[xs].reshape(K * own_degrees, width),
            order[xs * width : (xs + 1) * width],
            preferred_element_type=f32,
        )
    rows, wide = K * own_degrees, ordered32.shape[1]
    pieces = 2 * half // wide
    for piece in range(pieces):
        ordered32[piece * rows : (piece + 1) * rows] = ordered[:, piece * wide : (piece + 1) * wide]
    for l in range(own_degrees):
        parts = [
            ordered32[pl.ds(piece * rows + l, K, stride=own_degrees), :] for piece in range(pieces)
        ]
        forced = jnp.concatenate(
            [
                jnp.concatenate(parts[: pieces // 2], axis=1),
                jnp.concatenate(parts[pieces // 2 :], axis=1),
            ],
            axis=0,
        )
        out_ref[l] = own_part[l] + lax.dot_general(
            forced.astype(bf16), operator16[l], NT, preferred_element_type=f32
        )

    for d in range(1, X):
        pltpu.make_async_copy(p_all.at[x], p_all.at[x], x_send_sems.at[d - 1]).wait()
    for buffer, sem in ((p_send, p_send_sem), (f_send, f_sems.at[0]), (s_send, s_sems.at[0])):
        sent = buffer.at[pl.ds(0, buffer.shape[0] - 1)]
        pltpu.make_async_copy(sent, sent, sem).wait()


def shards(sizes, warming, table, thermal, operator):
    X, Y, A, B, C = sizes
    K = Y * A
    M = table.shape[0]
    own_levels, bands, longitudes = warming.shape
    own_degrees = table.shape[2]
    degrees = own_degrees * X * K
    levels = thermal.shape[3]
    lanes = 128
    vmem = pltpu.VMEM
    dma = pltpu.SemaphoreType.DMA
    table = jnp.transpose(table, (1, 2, 0))
    analysis = analysis_rows(M, degrees // M, longitudes)
    order = level_order(X, K, own_levels)
    result = pl.pallas_call(
        functools.partial(kernel, sizes),
        out_shape=jax.ShapeDtypeStruct((own_degrees, 2 * K, levels), f32),
        in_specs=[pl.BlockSpec(memory_space=pl.ANY)] * 6,
        out_specs=pl.BlockSpec(memory_space=pltpu.VMEM),
        scratch_shapes=[
            vmem(warming.shape, bf16),
            vmem(table.shape, bf16),
            vmem(thermal.shape, f32),
            vmem(operator.shape, f32),
            vmem(analysis.shape, bf16),
            vmem(order.shape, bf16),
            vmem((bands * own_degrees, M), f32),
            vmem((M * own_degrees, lanes), f32),
            vmem((M, 2 * own_levels, lanes), bf16),
            vmem((M, 2 * own_levels, lanes), bf16),
            vmem((M, own_degrees, lanes), bf16),
            vmem((X, M, own_degrees, lanes), bf16),
            vmem((X * K, own_degrees, K * 2 * own_levels), bf16),
            vmem((X, K, own_degrees, K * 2 * own_levels), bf16),
            vmem(operator.shape, bf16),
            vmem((own_degrees, 2 * K, levels), f32),
            vmem((2 * levels // min(lanes, levels) * K * own_degrees, min(lanes, levels)), f32),
            dma((6,)), dma((2,)), dma, dma((B * C,)), dma((X - 1,)), dma((X - 1,)), dma((2,)),
            pltpu.SemaphoreType.REGULAR,
        ],
        compiler_params=pltpu.CompilerParams(
            collective_id=0, has_side_effects=True, vmem_limit_bytes=60 * 2**20
        ),
        cost_estimate=pl.CostEstimate(flops=10**9, bytes_accessed=10**7, transcendentals=0),
    )(warming, table, thermal, operator, analysis, order)
    return jnp.transpose(result.reshape(own_degrees, 2, K, levels), (0, 2, 1, 3))


def build(mesh, sizes):
    finer = Mesh(mesh.devices.reshape(sizes), ("x", "y", "a", "b", "c"))
    shell, lat = ("x", "y", "a"), ("b", "c")
    in_specs = (
        P(shell, lat, None),
        P(None, lat, shell),
        P(shell, lat, None, None),
        P(shell, None, None),
    )
    return jax.shard_map(
        functools.partial(shards, sizes), mesh=finer, in_specs=in_specs,
        out_specs=P(shell, lat, None, None), check_vma=False,
    )


def solution(mesh):
    return build(mesh, (4, 8, 2, 4, 2))
```

```python
import functools
import math

import jax
import jax.numpy as jnp
import numpy as np
from jax import lax
from jax.experimental import pallas as pl
from jax.experimental.pallas import tpu as pltpu
from jax.sharding import Mesh, PartitionSpec as P

backward_euler_update = 0.5
MESH = pl.DeviceIdType.MESH
NT = (((1,), (1,)), ((), ()))
f32, bf16 = jnp.float32, jnp.bfloat16


def analysis_rows(orders, stride, longitudes):
    phase = (np.arange(orders)[:, None] * stride * np.arange(longitudes)[None, :]) % longitudes
    angles = phase.astype(np.float32) * np.float32(2.0 * math.pi / longitudes)
    stacked = np.stack([np.cos(angles), -np.sin(angles)], axis=0) / np.float32(longitudes)
    return jnp.asarray(stacked.reshape(2 * orders, longitudes)).astype(bf16)


def level_order(xs, ks, own_levels):
    n = xs * ks * 2 * own_levels
    x, k, c, r = np.unravel_index(np.arange(n), (xs, ks, 2, own_levels))
    matrix = np.zeros((n, n), np.float32)
    matrix[np.arange(n), np.ravel_multi_index((c, x, k, r), (2, xs, ks, own_levels))] = backward_euler_update
    return jnp.asarray(matrix).astype(bf16)


def split(value):
    high = value.astype(bf16)
    return high, (value - high.astype(f32)).astype(bf16)


def kernel(
    sizes,
    warm_hbm, table_hbm, thermal_hbm, operator_hbm, analysis_hbm, order_hbm,
    out_ref,
    warm, table, thermal, operator, analysis, order,
    rows32, turned32, f_send, f_all, p_send, p_recv, s_send, s_recv, operator16, own_part, ordered32,
    load_sems, p_sems, f_send_sem, f_sems, x_send_sem, x_recv_sems, far_sem, s_sems, plane_sem,
):
    X, Y, A, B, C = sizes
    K = Y * A
    M = B * C * K
    x, y, a = lax.axis_index("x"), lax.axis_index("y"), lax.axis_index("a")
    b, c = lax.axis_index("b"), lax.axis_index("c")
    k = y * A + a
    me = (b * C + c) * K + k
    own_levels, bands, longitudes = warm.shape
    own_degrees = table.shape[1]
    lanes = f_send.shape[2]

    def owner(m):
        return {
            "b": m // (C * K), "c": lax.rem(m // K, C),
            "y": lax.rem(m, K) // A, "a": lax.rem(m, A),
        }

    loads = [
        pltpu.make_async_copy(src, dst, load_sems.at[i])
        for i, (src, dst) in enumerate((
            (table_hbm, table), (warm_hbm, warm), (analysis_hbm, analysis),
            (thermal_hbm, thermal), (operator_hbm, operator), (order_hbm, order),
        ))
    ]
    for load in loads:
        load.start()

    barrier = pltpu.get_barrier_semaphore()

    def plane(dy, da, db, dc):
        return {
            "y": lax.rem(y + dy, Y), "a": lax.rem(a + da, A),
            "b": lax.rem(b + db, B), "c": lax.rem(c + dc, C),
        }

    columns = [(0, da, db, dc) for da in range(A) for db in range(B) for dc in range(C)][1:]
    rows = [(dy, 0, 0, 0) for dy in range(1, Y)]
    for step in columns + rows:
        pl.semaphore_signal(barrier, inc=1, device_id=plane(*step), device_id_type=MESH)
    for d in range(1, X):
        pl.semaphore_signal(
            barrier, inc=1, device_id={"x": lax.rem(x + d, X)}, device_id_type=MESH
        )

    loads[0].wait()
    rows32[...] = table[...].astype(f32).reshape(bands * own_degrees, M)
    for l in range(own_degrees):
        part = rows32[pl.ds(l, bands, stride=own_degrees), :]
        part = jnp.concatenate([part, jnp.zeros((lanes - bands, M), f32)], axis=0)
        turned32[pl.ds(l, M, stride=own_degrees), :] = part.T
    p_send[...] = turned32[...].reshape(M, own_degrees, lanes).astype(bf16)

    pl.semaphore_wait(barrier, len(columns) + len(rows) + X - 1)
    for step in rows:
        pl.semaphore_signal(plane_sem, inc=1, device_id=plane(*step), device_id_type=MESH)

    loads[1].wait()
    loads[2].wait()
    for r in range(own_levels):
        part = lax.dot_general(analysis[...], warm[r], NT, preferred_element_type=f32)
        part = jnp.concatenate([part, jnp.zeros((2 * M, lanes - bands), f32)], axis=1)
        for half in range(2):
            turned32[pl.ds(half * own_levels + r, M, stride=2 * own_levels), :] = part[
                half * M : (half + 1) * M
            ]
    f_send[...] = turned32[...].reshape(M, 2 * own_levels, lanes).astype(bf16)

    pl.semaphore_wait(plane_sem, len(rows))

    def f_copy(m, chunk):
        return pltpu.make_async_remote_copy(
            src_ref=f_send.at[m], dst_ref=f_all.at[x, me],
            send_sem=f_send_sem, recv_sem=f_sems.at[chunk],
            device_id=owner(m), device_id_type=MESH,
        )

    def p_copy(m, chunk):
        return pltpu.make_async_remote_copy(
            src_ref=p_send.at[m], dst_ref=p_recv.at[me],
            send_sem=p_sems.at[0], recv_sem=p_sems.at[1],
            device_id=owner(m), device_id_type=MESH,
        )

    chunks = sorted(
        ((db, dc) for db in range(B) for dc in range(C)),
        key=lambda step: min(step[0], B - step[0]),
    )

    def band_at(sign, chunk):
        db, dc = chunks[chunk]
        return lax.rem(b + sign * db + B, B) * C + lax.rem(c + sign * dc + C, C)

    def send_band(copy, chunk):
        band = band_at(1, chunk)

        def send(i, carry):
            copy(band * K + lax.rem(k + i, K), chunk).start()
            return carry

        lax.fori_loop(1 if chunk == 0 else 0, K, send, 0)

    pltpu.make_async_copy(f_send.at[me], f_all.at[x, me], f_sems.at[0]).start()
    for chunk in range(B * C):
        send_band(f_copy, chunk)
    pltpu.make_async_copy(p_send.at[me], p_recv.at[me], p_sems.at[1]).start()
    for chunk in range(B * C):
        send_band(p_copy, chunk)

    loads[3].wait()
    loads[4].wait()
    for l in range(own_degrees):
        high, low = split(operator[l])
        operator16[l] = high
        t_high, t_low = split(
            jnp.concatenate([thermal[l, :, half, :] for half in range(2)], axis=0)
        )
        own_part[l] = (
            lax.dot_general(t_high, high, NT, preferred_element_type=f32)
            + lax.dot_general(t_low, high, NT, preferred_element_type=f32)
            + lax.dot_general(t_high, low, NT, preferred_element_type=f32)
        )
    loads[5].wait()

    right, left = lax.rem(x + 1, X), lax.rem(x + X - 1, X)
    far = lax.rem(x + 2, X)

    def block(source, chunk):
        return f_all.at[source, pl.ds(band_at(-1, chunk) * K, K)]

    def pass_on(source, chunk, target, sem):
        pltpu.make_async_remote_copy(
            src_ref=block(source, chunk), dst_ref=block(source, chunk),
            send_sem=x_send_sem, recv_sem=sem,
            device_id={"x": target}, device_id_type=MESH,
        ).start()

    def arrived(source, chunk, sem):
        pltpu.make_async_copy(block(source, chunk), block(source, chunk), sem).wait()

    def hop(chunk):
        if chunk < B * C // 2:
            arrived(left, chunk, x_recv_sems.at[0, chunk])
            pass_on(left, chunk, right, far_sem)
        else:
            arrived(right, chunk, x_recv_sems.at[1, chunk])
            pass_on(right, chunk, left, far_sem)

    lag = min(5, B * C)
    for chunk in range(B * C):
        arrived(x, chunk, f_sems.at[chunk])
        pass_on(x, chunk, right, x_recv_sems.at[0, chunk])
        pass_on(x, chunk, left, x_recv_sems.at[1, chunk])
        if chunk >= lag:
            hop(chunk - lag)
    for chunk in range(B * C - lag, B * C):
        hop(chunk)
    for chunk in range(B * C):
        if chunk < B * C // 2:
            arrived(right, chunk, x_recv_sems.at[1, chunk])
        else:
            arrived(left, chunk, x_recv_sems.at[0, chunk])
    pltpu.make_async_copy(f_all.at[far], f_all.at[far], far_sem).wait()
    pltpu.make_async_copy(p_recv, p_recv, p_sems.at[1]).wait()

    width = X * K * 2 * own_levels
    total = jnp.zeros((K * own_degrees, width), f32)
    for band in range(B * C):
        here = pl.ds(band * K, K)
        total += lax.dot_general(
            p_recv[here].reshape(K * own_degrees, lanes),
            f_all[:, here].reshape(width, lanes),
            NT, preferred_element_type=f32,
        )
    s_send[...] = total.reshape(K, own_degrees, width).astype(bf16)

    def send_s(i, carry):
        target = lax.rem(k + i, K)
        pltpu.make_async_remote_copy(
            src_ref=s_send.at[target], dst_ref=s_recv.at[k],
            send_sem=s_sems.at[0], recv_sem=s_sems.at[1],
            device_id={"y": target // A, "a": lax.rem(target, A)}, device_id_type=MESH,
        ).start()
        return carry

    pltpu.make_async_copy(s_send.at[k], s_recv.at[k], s_sems.at[1]).start()
    lax.fori_loop(1, K, send_s, 0)
    pltpu.make_async_copy(s_recv, s_recv, s_sems.at[1]).wait()

    half = width // 2
    ordered = jnp.dot(
        s_recv[...].reshape(K * own_degrees, width), order[...], preferred_element_type=f32
    )
    rows, wide = K * own_degrees, ordered32.shape[1]
    pieces = 2 * half // wide
    for piece in range(pieces):
        ordered32[piece * rows : (piece + 1) * rows] = ordered[:, piece * wide : (piece + 1) * wide]
    for l in range(own_degrees):
        parts = [
            ordered32[pl.ds(piece * rows + l, K, stride=own_degrees), :] for piece in range(pieces)
        ]
        forced = jnp.concatenate(
            [
                jnp.concatenate(parts[: pieces // 2], axis=1),
                jnp.concatenate(parts[pieces // 2 :], axis=1),
            ],
            axis=0,
        )
        out_ref[l] = own_part[l] + lax.dot_general(
            forced.astype(bf16), operator16[l], NT, preferred_element_type=f32
        )

    for _ in range(X - 1):
        pltpu.make_async_copy(f_all.at[x], f_all.at[x], x_send_sem).wait()
    for buffer, sem in ((f_send, f_send_sem), (p_send, p_sems.at[0]), (s_send, s_sems.at[0])):
        sent = buffer.at[pl.ds(0, buffer.shape[0] - 1)]
        pltpu.make_async_copy(sent, sent, sem).wait()


def shards(sizes, warming, table, thermal, operator):
    X, Y, A, B, C = sizes
    K = Y * A
    M = table.shape[0]
    own_levels, bands, longitudes = warming.shape
    own_degrees = table.shape[2]
    degrees = own_degrees * X * K
    levels = thermal.shape[3]
    lanes = 128
    vmem = pltpu.VMEM
    dma = pltpu.SemaphoreType.DMA
    table = jnp.transpose(table, (1, 2, 0))
    analysis = analysis_rows(M, degrees // M, longitudes)
    order = level_order(X, K, own_levels)
    operands = (warming, table, thermal, operator, analysis, order)
    result = pl.pallas_call(
        functools.partial(kernel, sizes),
        out_shape=jax.ShapeDtypeStruct((own_degrees, 2 * K, levels), f32),
        in_specs=[pl.BlockSpec(memory_space=pl.ANY)] * 6,
        out_specs=pl.BlockSpec(memory_space=pltpu.VMEM),
        scratch_shapes=[
            vmem(warming.shape, bf16),
            vmem(table.shape, bf16),
            vmem(thermal.shape, f32),
            vmem(operator.shape, f32),
            vmem(analysis.shape, bf16),
            vmem(order.shape, bf16),
            vmem((bands * own_degrees, M), f32),
            vmem((M * own_degrees, lanes), f32),
            vmem((M, 2 * own_levels, lanes), bf16),
            vmem((X, M, 2 * own_levels, lanes), bf16),
            vmem((M, own_degrees, lanes), bf16),
            vmem((M, own_degrees, lanes), bf16),
            vmem((K, own_degrees, 2 * levels), bf16),
            vmem((K, own_degrees, 2 * levels), bf16),
            vmem(operator.shape, bf16),
            vmem((own_degrees, 2 * K, levels), f32),
            vmem((2 * levels // min(lanes, levels) * K * own_degrees, min(lanes, levels)), f32),
            dma((6,)), dma((2,)), dma, dma((B * C,)), dma, dma((2, B * C)), dma, dma((2,)),
            pltpu.SemaphoreType.REGULAR,
        ],
        compiler_params=pltpu.CompilerParams(
            collective_id=0, has_side_effects=True, vmem_limit_bytes=40 * 2**20
        ),
        cost_estimate=pl.CostEstimate(flops=10**9, bytes_accessed=10**7, transcendentals=0),
    )(*(pltpu.with_memory_space_constraint(v, pltpu.HBM) for v in operands))
    return jnp.transpose(result.reshape(own_degrees, 2, K, levels), (0, 2, 1, 3))


def build(mesh, sizes):
    finer = Mesh(mesh.devices.reshape(sizes), ("x", "y", "a", "b", "c"))
    shell, lat = ("x", "y", "a"), ("b", "c")
    in_specs = (
        P(shell, lat, None),
        P(None, lat, shell),
        P(shell, lat, None, None),
        P(shell, None, None),
    )
    return jax.shard_map(
        functools.partial(shards, sizes), mesh=finer, in_specs=in_specs,
        out_specs=P(shell, lat, None, None), check_vma=False,
    )


def solution(mesh):
    return build(mesh, (4, 8, 2, 4, 2))
```

```python
import functools
import math

import jax
import jax.numpy as jnp
import numpy as np
from jax import lax
from jax.experimental import pallas as pl
from jax.experimental.pallas import tpu as pltpu
from jax.sharding import Mesh, PartitionSpec as P

backward_euler_update = 0.5
MESH = pl.DeviceIdType.MESH
NT = (((1,), (1,)), ((), ()))
f32, bf16 = jnp.float32, jnp.bfloat16


def analysis_rows(orders, stride, longitudes):
    phase = (np.arange(orders)[:, None] * stride * np.arange(longitudes)[None, :]) % longitudes
    angles = phase.astype(np.float32) * np.float32(2.0 * math.pi / longitudes)
    stacked = np.stack([np.cos(angles), -np.sin(angles)], axis=1) / np.float32(longitudes)
    return jnp.asarray(stacked.reshape(2 * orders, longitudes)).astype(bf16)


def level_order(xs, ks, own_levels):
    n = xs * ks * 2 * own_levels
    x, r, k, c = np.unravel_index(np.arange(n), (xs, own_levels, ks, 2))
    matrix = np.zeros((n, n), np.float32)
    matrix[np.arange(n), np.ravel_multi_index((c, x, k, r), (2, xs, ks, own_levels))] = backward_euler_update
    return jnp.asarray(matrix).astype(bf16)


def split(value):
    high = value.astype(bf16)
    return high, (value - high.astype(f32)).astype(bf16)


def kernel(
    sizes,
    warm_hbm, table_hbm, thermal_hbm, operator_hbm, analysis_hbm, order_hbm,
    out_ref,
    warm, table, thermal, operator, analysis, order,
    rows32, turned32, total32, p_rows, f_send, f_all, p_send, p_recv, s_send, s_recv, operator16, own_part, ordered32,
    load_sems, p_sems, f_send_sem, f_sems, x_send_sem, x_recv_sems, far_sem, s_sems, plane_sem,
):
    X, Y, A, B, C = sizes
    K = Y * A
    M = B * C * K
    x, y, a = lax.axis_index("x"), lax.axis_index("y"), lax.axis_index("a")
    b, c = lax.axis_index("b"), lax.axis_index("c")
    k = y * A + a
    me = (b * C + c) * K + k
    own_levels, bands, longitudes = warm.shape
    own_degrees = table.shape[1]
    tiles = f_send.shape[1]

    def owner(m):
        return {
            "b": m // (C * K), "c": lax.rem(m // K, C),
            "y": lax.rem(m, K) // A, "a": lax.rem(m, A),
        }

    loads = [
        pltpu.make_async_copy(src, dst, load_sems.at[i])
        for i, (src, dst) in enumerate((
            (table_hbm, table), (warm_hbm, warm), (analysis_hbm, analysis),
            (thermal_hbm, thermal), (operator_hbm, operator), (order_hbm, order),
        ))
    ]
    for load in loads:
        load.start()

    barrier = pltpu.get_barrier_semaphore()

    def plane(dy, da, db, dc):
        return {
            "y": lax.rem(y + dy, Y), "a": lax.rem(a + da, A),
            "b": lax.rem(b + db, B), "c": lax.rem(c + dc, C),
        }

    columns = [(0, da, db, dc) for da in range(A) for db in range(B) for dc in range(C)][1:]
    rows = [(dy, 0, 0, 0) for dy in range(1, Y)]
    for step in columns + rows:
        pl.semaphore_signal(barrier, inc=1, device_id=plane(*step), device_id_type=MESH)
    for d in range(1, X):
        pl.semaphore_signal(
            barrier, inc=1, device_id={"x": lax.rem(x + d, X)}, device_id_type=MESH
        )

    loads[0].wait()
    rows32[...] = table[...].astype(f32).reshape(bands * own_degrees, M)
    for half in range(2):
        wide = jnp.concatenate(
            [
                rows32[pl.ds(l, bands, stride=own_degrees), :].T
                for l in range(half * own_degrees // 2, (half + 1) * own_degrees // 2)
            ],
            axis=1,
        )
        for tile in range(tiles):
            turned32[tile, pl.ds(half, M, stride=2), :] = wide[:, tile * 128 : (tile + 1) * 128]
    for tile in range(tiles):
        p_send[:, tile] = turned32[tile].reshape(M, 2, 128).astype(bf16)

    pl.semaphore_wait(barrier, len(columns) + len(rows) + X - 1)
    for step in rows:
        pl.semaphore_signal(plane_sem, inc=1, device_id=plane(*step), device_id_type=MESH)

    loads[1].wait()
    loads[2].wait()
    fourier = lax.dot_general(
        analysis[...], warm[...].reshape(own_levels * bands, longitudes), NT,
        preferred_element_type=f32,
    )
    for tile in range(tiles):
        f_send[:, tile] = (
            fourier[:, tile * 128 : (tile + 1) * 128].reshape(M, 2, 128).astype(bf16)
        )

    pl.semaphore_wait(plane_sem, len(rows))

    def f_copy(m, chunk):
        return pltpu.make_async_remote_copy(
            src_ref=f_send.at[m], dst_ref=f_all.at[x, me],
            send_sem=f_send_sem, recv_sem=f_sems.at[chunk],
            device_id=owner(m), device_id_type=MESH,
        )

    def p_copy(m, chunk):
        return pltpu.make_async_remote_copy(
            src_ref=p_send.at[m], dst_ref=p_recv.at[me],
            send_sem=p_sems.at[0], recv_sem=p_sems.at[1],
            device_id=owner(m), device_id_type=MESH,
        )

    chunks = sorted(
        ((db, dc) for db in range(B) for dc in range(C)),
        key=lambda step: min(step[0], B - step[0]),
    )

    def band_at(sign, chunk):
        db, dc = chunks[chunk]
        return lax.rem(b + sign * db + B, B) * C + lax.rem(c + sign * dc + C, C)

    def send_band(copy, chunk):
        band = band_at(1, chunk)

        def send(i, carry):
            copy(band * K + lax.rem(k + i, K), chunk).start()
            return carry

        lax.fori_loop(1 if chunk == 0 else 0, K, send, 0)

    pltpu.make_async_copy(f_send.at[me], f_all.at[x, me], f_sems.at[0]).start()
    for chunk in range(B * C):
        send_band(f_copy, chunk)
    pltpu.make_async_copy(p_send.at[me], p_recv.at[me], p_sems.at[1]).start()
    for chunk in range(B * C):
        send_band(p_copy, chunk)

    loads[3].wait()
    loads[4].wait()
    for l in range(own_degrees):
        high, low = split(operator[l])
        operator16[l] = high
        t_high, t_low = split(
            jnp.concatenate([thermal[l, :, half, :] for half in range(2)], axis=0)
        )
        own_part[l] = (
            lax.dot_general(t_high, high, NT, preferred_element_type=f32)
            + lax.dot_general(t_low, high, NT, preferred_element_type=f32)
            + lax.dot_general(t_high, low, NT, preferred_element_type=f32)
        )
    loads[5].wait()

    right, left = lax.rem(x + 1, X), lax.rem(x + X - 1, X)
    far = lax.rem(x + 2, X)

    def block(source, chunk):
        return f_all.at[source, pl.ds(band_at(-1, chunk) * K, K)]

    def pass_on(source, chunk, target, sem):
        pltpu.make_async_remote_copy(
            src_ref=block(source, chunk), dst_ref=block(source, chunk),
            send_sem=x_send_sem, recv_sem=sem,
            device_id={"x": target}, device_id_type=MESH,
        ).start()

    def arrived(source, chunk, sem):
        pltpu.make_async_copy(block(source, chunk), block(source, chunk), sem).wait()

    def hop(chunk):
        if chunk < B * C // 2:
            arrived(left, chunk, x_recv_sems.at[0, chunk])
            pass_on(left, chunk, right, far_sem)
        else:
            arrived(right, chunk, x_recv_sems.at[1, chunk])
            pass_on(right, chunk, left, far_sem)

    lag = min(8, B * C)
    for chunk in range(B * C):
        arrived(x, chunk, f_sems.at[chunk])
        pass_on(x, chunk, right, x_recv_sems.at[0, chunk])
        pass_on(x, chunk, left, x_recv_sems.at[1, chunk])
        if chunk >= lag:
            hop(chunk - lag)
    for chunk in range(B * C - lag, B * C):
        hop(chunk)
    def spread(buffer, parts):
        wide = jnp.concatenate(
            [buffer[:, tile].reshape(2 * K, 128) for tile in range(tiles)], axis=1
        )
        return jnp.concatenate(
            [wide[:, part * bands : (part + 1) * bands] for part in range(parts)], axis=0
        )

    width = K * 2 * own_levels
    rows = K * own_degrees

    def spectrum(source):
        total = jnp.zeros((rows, width), f32)
        for band in range(B * C):
            here = pl.ds(band * K, K)
            total += lax.dot_general(
                p_rows[band], spread(f_all.at[source, here], own_levels), NT,
                preferred_element_type=f32,
            )
        for l in range(own_degrees // 2):
            total32[pl.ds(l, 2 * K, stride=own_degrees // 2), :] = total[
                l * 2 * K : (l + 1) * 2 * K
            ]
        s_send[source] = total32[...].reshape(K, own_degrees, width).astype(bf16)

        def send(i, carry):
            target = lax.rem(k + i, K)
            pltpu.make_async_remote_copy(
                src_ref=s_send.at[source, target], dst_ref=s_recv.at[source, k],
                send_sem=s_sems.at[0], recv_sem=s_sems.at[1],
                device_id={"y": target // A, "a": lax.rem(target, A)}, device_id_type=MESH,
            ).start()
            return carry

        pltpu.make_async_copy(s_send.at[source, k], s_recv.at[source, k], s_sems.at[1]).start()
        lax.fori_loop(1, K, send, 0)

    pltpu.make_async_copy(p_recv, p_recv, p_sems.at[1]).wait()
    for band in range(B * C):
        p_rows[band] = spread(p_recv.at[pl.ds(band * K, K)], own_degrees // 2)
    spectrum(x)
    for chunk in range(B * C // 2, B * C):
        arrived(left, chunk, x_recv_sems.at[0, chunk])
    spectrum(left)
    for chunk in range(B * C // 2):
        arrived(right, chunk, x_recv_sems.at[1, chunk])
    spectrum(right)
    pltpu.make_async_copy(f_all.at[far], f_all.at[far], far_sem).wait()
    spectrum(far)
    pltpu.make_async_copy(s_recv, s_recv, s_sems.at[1]).wait()

    half = X * K * own_levels
    ordered = jnp.zeros((rows, 2 * half), f32)
    for source in range(X):
        ordered += jnp.dot(
            s_recv[source].reshape(rows, width),
            order[source * width : (source + 1) * width],
            preferred_element_type=f32,
        )
    wide = ordered32.shape[1]
    pieces = 2 * half // wide
    for piece in range(pieces):
        ordered32[piece * rows : (piece + 1) * rows] = ordered[:, piece * wide : (piece + 1) * wide]
    for l in range(own_degrees):
        parts = [
            ordered32[pl.ds(piece * rows + l, K, stride=own_degrees), :] for piece in range(pieces)
        ]
        forced = jnp.concatenate(
            [
                jnp.concatenate(parts[: pieces // 2], axis=1),
                jnp.concatenate(parts[pieces // 2 :], axis=1),
            ],
            axis=0,
        )
        out_ref[l] = own_part[l] + lax.dot_general(
            forced.astype(bf16), operator16[l], NT, preferred_element_type=f32
        )

    for _ in range(X - 1):
        pltpu.make_async_copy(f_all.at[x], f_all.at[x], x_send_sem).wait()
    for buffer, sem in ((f_send, f_send_sem), (p_send, p_sems.at[0])):
        sent = buffer.at[pl.ds(0, M - 1)]
        pltpu.make_async_copy(sent, sent, sem).wait()
    sent = s_send.at[:, pl.ds(0, K - 1)]
    pltpu.make_async_copy(sent, sent, s_sems.at[0]).wait()


def shards(sizes, warming, table, thermal, operator):
    X, Y, A, B, C = sizes
    K = Y * A
    M = table.shape[0]
    own_levels, bands, longitudes = warming.shape
    own_degrees = table.shape[2]
    degrees = own_degrees * X * K
    levels = thermal.shape[3]
    lanes = 128
    tiles = own_levels * bands // lanes
    vmem = pltpu.VMEM
    dma = pltpu.SemaphoreType.DMA
    table = jnp.transpose(table, (1, 2, 0))
    analysis = analysis_rows(M, degrees // M, longitudes)
    order = level_order(X, K, own_levels)
    operands = (warming, table, thermal, operator, analysis, order)
    result = pl.pallas_call(
        functools.partial(kernel, sizes),
        out_shape=jax.ShapeDtypeStruct((own_degrees, 2 * K, levels), f32),
        in_specs=[pl.BlockSpec(memory_space=pl.ANY)] * 6,
        out_specs=pl.BlockSpec(memory_space=pltpu.VMEM),
        scratch_shapes=[
            vmem(warming.shape, bf16),
            vmem(table.shape, bf16),
            vmem(thermal.shape, f32),
            vmem(operator.shape, f32),
            vmem(analysis.shape, bf16),
            vmem(order.shape, bf16),
            vmem((bands * own_degrees, M), f32),
            vmem((tiles, 2 * M, lanes), f32),
            vmem((K * own_degrees, 2 * levels // X), f32),
            vmem((B * C, K * own_degrees, bands), bf16),
            vmem((M, tiles, 2, lanes), bf16),
            vmem((X, M, tiles, 2, lanes), bf16),
            vmem((M, tiles, 2, lanes), bf16),
            vmem((M, tiles, 2, lanes), bf16),
            vmem((X, K, own_degrees, 2 * levels // X), bf16),
            vmem((X, K, own_degrees, 2 * levels // X), bf16),
            vmem(operator.shape, bf16),
            vmem((own_degrees, 2 * K, levels), f32),
            vmem((2 * levels // min(lanes, levels) * K * own_degrees, min(lanes, levels)), f32),
            dma((6,)), dma((2,)), dma, dma((B * C,)), dma, dma((2, B * C)), dma, dma((2,)),
            pltpu.SemaphoreType.REGULAR,
        ],
        compiler_params=pltpu.CompilerParams(
            collective_id=0, has_side_effects=True, vmem_limit_bytes=40 * 2**20
        ),
        cost_estimate=pl.CostEstimate(flops=10**9, bytes_accessed=10**7, transcendentals=0),
    )(*(pltpu.with_memory_space_constraint(v, pltpu.HBM) for v in operands))
    return jnp.transpose(result.reshape(own_degrees, 2, K, levels), (0, 2, 1, 3))


def build(mesh, sizes):
    finer = Mesh(mesh.devices.reshape(sizes), ("x", "y", "a", "b", "c"))
    shell, lat = ("x", "y", "a"), ("b", "c")
    in_specs = (
        P(shell, lat, None),
        P(None, lat, shell),
        P(shell, lat, None, None),
        P(shell, None, None),
    )
    return jax.shard_map(
        functools.partial(shards, sizes), mesh=finer, in_specs=in_specs,
        out_specs=P(shell, lat, None, None), check_vma=False,
    )


def solution(mesh):
    return build(mesh, (4, 8, 2, 4, 2))
```

```python
import functools
import math

import jax
import jax.numpy as jnp
import numpy as np
from jax import lax
from jax.experimental import pallas as pl
from jax.experimental.pallas import tpu as pltpu
from jax.sharding import Mesh, PartitionSpec as P

backward_euler_update = 0.5
MESH = pl.DeviceIdType.MESH
NT = (((1,), (1,)), ((), ()))
f32, bf16 = jnp.float32, jnp.bfloat16


def analysis_rows(orders, stride, longitudes):
    phase = (np.arange(orders)[:, None] * stride * np.arange(longitudes)[None, :]) % longitudes
    angles = phase.astype(np.float32) * np.float32(2.0 * math.pi / longitudes)
    stacked = np.stack([np.cos(angles), -np.sin(angles)], axis=1) / np.float32(longitudes)
    return jnp.asarray(stacked.reshape(2 * orders, longitudes)).astype(bf16)


def level_order(xs, ks, own_levels):
    n = xs * ks * 2 * own_levels
    x, r, k, c = np.unravel_index(np.arange(n), (xs, own_levels, ks, 2))
    matrix = np.zeros((n, n), np.float32)
    matrix[np.arange(n), np.ravel_multi_index((c, x, k, r), (2, xs, ks, own_levels))] = backward_euler_update
    return jnp.asarray(matrix).astype(bf16)


def split(value):
    high = value.astype(bf16)
    return high, (value - high.astype(f32)).astype(bf16)


def kernel(
    sizes,
    warm_hbm, table_hbm, thermal_hbm, operator_hbm, analysis_hbm, order_hbm,
    out_ref,
    warm, table, thermal, operator, analysis, order,
    rows32, turned32, total32, p_rows, f_send, f_pair, f_all, p_send, p_pair, p_recv, s_send, s_recv, operator16, own_part, ordered32,
    load_sems, f_pair_sems, p_pair_sems, p_sems, f_send_sem, f_sems, x_send_sem, x_recv_sems, far_sem, s_sems, plane_sem,
):
    X, Y, A, B, C = sizes
    K = Y * A
    M = B * C * K
    x, y, a = lax.axis_index("x"), lax.axis_index("y"), lax.axis_index("a")
    b, c = lax.axis_index("b"), lax.axis_index("c")
    k = y * A + a
    own_levels, bands, longitudes = warm.shape
    own_degrees = table.shape[1]
    tiles = f_send.shape[3]

    loads = [
        pltpu.make_async_copy(src, dst, load_sems.at[i])
        for i, (src, dst) in enumerate((
            (table_hbm, table), (warm_hbm, warm), (analysis_hbm, analysis),
            (thermal_hbm, thermal), (operator_hbm, operator), (order_hbm, order),
        ))
    ]
    for load in loads:
        load.start()

    barrier = pltpu.get_barrier_semaphore()

    def plane(dy, da, db, dc):
        return {
            "y": lax.rem(y + dy, Y), "a": lax.rem(a + da, A),
            "b": lax.rem(b + db, B), "c": lax.rem(c + dc, C),
        }

    columns = [(0, da, db, dc) for da in range(A) for db in range(B) for dc in range(C)][1:]
    rows = [(dy, 0, 0, 0) for dy in range(1, Y)]
    columns.sort(key=lambda step: -min(A * step[2] + step[1], A * B - A * step[2] - step[1]))
    rows.sort(key=lambda step: -min(step[0], Y - step[0]))
    for step in columns + rows:
        pl.semaphore_signal(barrier, inc=1, device_id=plane(*step), device_id_type=MESH)
    for d in range(1, X):
        pl.semaphore_signal(
            barrier, inc=1, device_id={"x": lax.rem(x + d, X)}, device_id_type=MESH
        )

    loads[0].wait()
    rows32[...] = table[...].astype(f32).reshape(bands * own_degrees, M)
    for half in range(2):
        wide = jnp.concatenate(
            [
                rows32[pl.ds(l, bands, stride=own_degrees), :].T
                for l in range(half * own_degrees // 2, (half + 1) * own_degrees // 2)
            ],
            axis=1,
        )
        for tile in range(tiles):
            turned32[tile, pl.ds(half, M, stride=2), :] = wide[:, tile * 128 : (tile + 1) * 128]
    for tile in range(tiles):
        p_send[:, :, :, tile] = turned32[tile].reshape(B, C, K, 2, 128).astype(bf16)

    pl.semaphore_wait(barrier, len(columns) + len(rows) + X - 1)
    for step in rows:
        pl.semaphore_signal(plane_sem, inc=1, device_id=plane(*step), device_id_type=MESH)

    def pair(own, both, sems):
        for other in range(1, C):
            core = lax.rem(c + other, C)
            pltpu.make_async_remote_copy(
                src_ref=own.at[:, core], dst_ref=both.at[:, :, c],
                send_sem=sems.at[0], recv_sem=sems.at[1],
                device_id={"c": core}, device_id_type=MESH,
            ).start()
        pltpu.make_async_copy(own.at[:, c], both.at[:, :, c], sems.at[1]).start()

    pair(p_send, p_pair, p_pair_sems)

    loads[1].wait()
    loads[2].wait()
    fourier = lax.dot_general(
        analysis[...], warm[...].reshape(own_levels * bands, longitudes), NT,
        preferred_element_type=f32,
    )
    for tile in range(tiles):
        f_send[:, :, :, tile] = (
            fourier[:, tile * 128 : (tile + 1) * 128].reshape(B, C, K, 2, 128).astype(bf16)
        )

    pair(f_send, f_pair, f_pair_sems)
    pl.semaphore_wait(plane_sem, len(rows))

    def f_copy(target_b, target_k, chunk):
        return pltpu.make_async_remote_copy(
            src_ref=f_pair.at[target_b, target_k], dst_ref=f_all.at[x, b, k],
            send_sem=f_send_sem, recv_sem=f_sems.at[chunk],
            device_id={"y": target_k // A, "a": lax.rem(target_k, A), "b": target_b},
            device_id_type=MESH,
        )

    def p_copy(target_b, target_k, chunk):
        return pltpu.make_async_remote_copy(
            src_ref=p_pair.at[target_b, target_k], dst_ref=p_recv.at[b, k],
            send_sem=p_sems.at[0], recv_sem=p_sems.at[1],
            device_id={"y": target_k // A, "a": lax.rem(target_k, A), "b": target_b},
            device_id_type=MESH,
        )

    chunks = sorted(range(B), key=lambda step: min(step, B - step))

    def place(sign, chunk):
        return lax.rem(b + sign * chunks[chunk] + B, B)

    def send_chunk(copy, chunk):
        target_b = place(1, chunk)

        def send(i, carry):
            copy(target_b, lax.rem(k + i, K), chunk).start()
            return carry

        lax.fori_loop(1 if chunk == 0 else 0, K, send, 0)

    pltpu.make_async_copy(f_pair, f_pair, f_pair_sems.at[1]).wait()
    pltpu.make_async_copy(f_pair.at[b, k], f_all.at[x, b, k], f_sems.at[0]).start()
    for chunk in range(B):
        send_chunk(f_copy, chunk)
    pltpu.make_async_copy(p_pair, p_pair, p_pair_sems.at[1]).wait()
    pltpu.make_async_copy(p_pair.at[b, k], p_recv.at[b, k], p_sems.at[1]).start()
    for chunk in range(B):
        send_chunk(p_copy, chunk)

    loads[3].wait()
    loads[4].wait()
    for l in range(own_degrees):
        high, low = split(operator[l])
        operator16[l] = high
        t_high, t_low = split(
            jnp.concatenate([thermal[l, :, half, :] for half in range(2)], axis=0)
        )
        own_part[l] = (
            lax.dot_general(t_high, high, NT, preferred_element_type=f32)
            + lax.dot_general(t_low, high, NT, preferred_element_type=f32)
            + lax.dot_general(t_high, low, NT, preferred_element_type=f32)
        )
    loads[5].wait()

    right, left = lax.rem(x + 1, X), lax.rem(x + X - 1, X)
    far = lax.rem(x + 2, X)

    def block(source, chunk):
        return f_all.at[source, place(-1, chunk)]

    def pass_on(source, chunk, target, sem):
        pltpu.make_async_remote_copy(
            src_ref=block(source, chunk), dst_ref=block(source, chunk),
            send_sem=x_send_sem, recv_sem=sem,
            device_id={"x": target}, device_id_type=MESH,
        ).start()

    def arrived(source, chunk, sem):
        pltpu.make_async_copy(block(source, chunk), block(source, chunk), sem).wait()

    for chunk in range(B):
        arrived(x, chunk, f_sems.at[chunk])
        pass_on(x, chunk, right, x_recv_sems.at[0, chunk])
        pass_on(x, chunk, left, x_recv_sems.at[1, chunk])
        pass_on(x, chunk, far, far_sem)

    def spread(buffer, core, parts):
        wide = jnp.concatenate(
            [buffer[:, core, tile].reshape(2 * K, 128) for tile in range(tiles)], axis=1
        )
        return jnp.concatenate(
            [wide[:, part * bands : (part + 1) * bands] for part in range(parts)], axis=0
        )

    width = K * 2 * own_levels
    rows = K * own_degrees

    def spectrum(source):
        total = jnp.zeros((rows, width), f32)
        for band in range(B * C):
            total += lax.dot_general(
                p_rows[band], spread(f_all.at[source, band // C], band % C, own_levels), NT,
                preferred_element_type=f32,
            )
        for l in range(own_degrees // 2):
            total32[pl.ds(l, 2 * K, stride=own_degrees // 2), :] = total[
                l * 2 * K : (l + 1) * 2 * K
            ]
        s_send[source] = total32[...].reshape(K, own_degrees, width).astype(bf16)

        def send(i, carry):
            target = lax.rem(k + i, K)
            pltpu.make_async_remote_copy(
                src_ref=s_send.at[source, target], dst_ref=s_recv.at[source, k],
                send_sem=s_sems.at[0], recv_sem=s_sems.at[1],
                device_id={"y": target // A, "a": lax.rem(target, A)}, device_id_type=MESH,
            ).start()
            return carry

        pltpu.make_async_copy(s_send.at[source, k], s_recv.at[source, k], s_sems.at[1]).start()
        lax.fori_loop(1, K, send, 0)

    pltpu.make_async_copy(p_recv, p_recv, p_sems.at[1]).wait()
    for band in range(B * C):
        p_rows[band] = spread(p_recv.at[band // C], band % C, own_degrees // 2)
    spectrum(x)
    for chunk in range(B):
        arrived(left, chunk, x_recv_sems.at[0, chunk])
    spectrum(left)
    for chunk in range(B):
        arrived(right, chunk, x_recv_sems.at[1, chunk])
    spectrum(right)
    pltpu.make_async_copy(f_all.at[far], f_all.at[far], far_sem).wait()
    spectrum(far)
    pltpu.make_async_copy(s_recv, s_recv, s_sems.at[1]).wait()

    half = X * K * own_levels
    ordered = jnp.zeros((rows, 2 * half), f32)
    for source in range(X):
        ordered += jnp.dot(
            s_recv[source].reshape(rows, width),
            order[source * width : (source + 1) * width],
            preferred_element_type=f32,
        )
    wide = ordered32.shape[1]
    pieces = 2 * half // wide
    for piece in range(pieces):
        ordered32[piece * rows : (piece + 1) * rows] = ordered[:, piece * wide : (piece + 1) * wide]
    for l in range(own_degrees):
        parts = [
            ordered32[pl.ds(piece * rows + l, K, stride=own_degrees), :] for piece in range(pieces)
        ]
        forced = jnp.concatenate(
            [
                jnp.concatenate(parts[: pieces // 2], axis=1),
                jnp.concatenate(parts[pieces // 2 :], axis=1),
            ],
            axis=0,
        )
        out_ref[l] = own_part[l] + lax.dot_general(
            forced.astype(bf16), operator16[l], NT, preferred_element_type=f32
        )

    for _ in range(X - 1):
        pltpu.make_async_copy(f_all.at[x], f_all.at[x], x_send_sem).wait()
    for both, sem in ((f_pair, f_send_sem), (p_pair, p_sems.at[0])):
        sent = both.at[:, pl.ds(0, K - 1)]
        pltpu.make_async_copy(sent, sent, sem).wait()
        sent = both.at[pl.ds(0, B - 1), K - 1]
        pltpu.make_async_copy(sent, sent, sem).wait()
    for own, sems in ((f_send, f_pair_sems), (p_send, p_pair_sems)):
        sent = own.at[:, pl.ds(0, C - 1)]
        pltpu.make_async_copy(sent, sent, sems.at[0]).wait()
    sent = s_send.at[:, pl.ds(0, K - 1)]
    pltpu.make_async_copy(sent, sent, s_sems.at[0]).wait()


def shards(sizes, warming, table, thermal, operator):
    X, Y, A, B, C = sizes
    K = Y * A
    M = table.shape[0]
    own_levels, bands, longitudes = warming.shape
    own_degrees = table.shape[2]
    degrees = own_degrees * X * K
    levels = thermal.shape[3]
    lanes = 128
    tiles = own_levels * bands // lanes
    vmem = pltpu.VMEM
    dma = pltpu.SemaphoreType.DMA
    table = jnp.transpose(table, (1, 2, 0))
    analysis = analysis_rows(M, degrees // M, longitudes)
    order = level_order(X, K, own_levels)
    operands = (warming, table, thermal, operator, analysis, order)
    result = pl.pallas_call(
        functools.partial(kernel, sizes),
        out_shape=jax.ShapeDtypeStruct((own_degrees, 2 * K, levels), f32),
        in_specs=[pl.BlockSpec(memory_space=pl.ANY)] * 6,
        out_specs=pl.BlockSpec(memory_space=pltpu.VMEM),
        scratch_shapes=[
            vmem(warming.shape, bf16),
            vmem(table.shape, bf16),
            vmem(thermal.shape, f32),
            vmem(operator.shape, f32),
            vmem(analysis.shape, bf16),
            vmem(order.shape, bf16),
            vmem((bands * own_degrees, M), f32),
            vmem((tiles, 2 * M, lanes), f32),
            vmem((K * own_degrees, 2 * levels // X), f32),
            vmem((B * C, K * own_degrees, bands), bf16),
            vmem((B, C, K, tiles, 2, lanes), bf16),
            vmem((B, K, C, tiles, 2, lanes), bf16),
            vmem((X, B, K, C, tiles, 2, lanes), bf16),
            vmem((B, C, K, tiles, 2, lanes), bf16),
            vmem((B, K, C, tiles, 2, lanes), bf16),
            vmem((B, K, C, tiles, 2, lanes), bf16),
            vmem((X, K, own_degrees, 2 * levels // X), bf16),
            vmem((X, K, own_degrees, 2 * levels // X), bf16),
            vmem(operator.shape, bf16),
            vmem((own_degrees, 2 * K, levels), f32),
            vmem((2 * levels // min(lanes, levels) * K * own_degrees, min(lanes, levels)), f32),
            dma((6,)), dma((2,)), dma((2,)), dma((2,)), dma, dma((B,)), dma, dma((2, B)), dma, dma((2,)),
            pltpu.SemaphoreType.REGULAR,
        ],
        compiler_params=pltpu.CompilerParams(
            collective_id=0, has_side_effects=True, vmem_limit_bytes=40 * 2**20
        ),
        cost_estimate=pl.CostEstimate(flops=10**9, bytes_accessed=10**7, transcendentals=0),
    )(*(pltpu.with_memory_space_constraint(v, pltpu.HBM) for v in operands))
    return jnp.transpose(result.reshape(own_degrees, 2, K, levels), (0, 2, 1, 3))


def build(mesh, sizes):
    finer = Mesh(mesh.devices.reshape(sizes), ("x", "y", "a", "b", "c"))
    shell, lat = ("x", "y", "a"), ("b", "c")
    in_specs = (
        P(shell, lat, None),
        P(None, lat, shell),
        P(shell, lat, None, None),
        P(shell, None, None),
    )
    return jax.shard_map(
        functools.partial(shards, sizes), mesh=finer, in_specs=in_specs,
        out_specs=P(shell, lat, None, None), check_vma=False,
    )


def solution(mesh):
    return build(mesh, (4, 8, 2, 4, 2))
```

```python
import functools
import math

import jax
import jax.numpy as jnp
import numpy as np
from jax import lax
from jax.experimental import pallas as pl
from jax.experimental.pallas import tpu as pltpu
from jax.sharding import Mesh, PartitionSpec as P

backward_euler_update = 0.5
MESH = pl.DeviceIdType.MESH
NT = (((1,), (1,)), ((), ()))
f32, bf16 = jnp.float32, jnp.bfloat16


def analysis_rows(orders, stride, longitudes):
    phase = (np.arange(orders)[:, None] * stride * np.arange(longitudes)[None, :]) % longitudes
    angles = phase.astype(np.float32) * np.float32(2.0 * math.pi / longitudes)
    stacked = np.stack([np.cos(angles), -np.sin(angles)], axis=1) / np.float32(longitudes)
    return jnp.asarray(stacked.reshape(2 * orders, longitudes)).astype(bf16)


def level_order(xs, ks, own_levels):
    n = xs * ks * 2 * own_levels
    x, r, k, c = np.unravel_index(np.arange(n), (xs, own_levels, ks, 2))
    matrix = np.zeros((n, n), np.float32)
    matrix[np.arange(n), np.ravel_multi_index((c, x, k, r), (2, xs, ks, own_levels))] = backward_euler_update
    return jnp.asarray(matrix).astype(bf16)


def split(value):
    high = value.astype(bf16)
    return high, (value - high.astype(f32)).astype(bf16)


def kernel(
    sizes,
    warm_hbm, table_hbm, thermal_hbm, operator_hbm, analysis_hbm, order_hbm,
    out_ref,
    warm, table, thermal, operator, analysis, order,
    rows32, turned32, total32, p_rows, f_send, f_pair, f_all, p_send, p_pair, p_recv, s_send, s_recv, operator16, own_part, ordered32,
    load_sems, f_pair_sems, p_pair_sems, p_sems, f_send_sem, f_sems, x_send_sem, x_recv_sems, far_sem, s_sems, plane_sem,
):
    X, Y, A, B, C = sizes
    K = Y * A
    M = B * C * K
    x, y, a = lax.axis_index("x"), lax.axis_index("y"), lax.axis_index("a")
    b, c = lax.axis_index("b"), lax.axis_index("c")
    k = y * A + a
    own_levels, bands, longitudes = warm.shape
    own_degrees = table.shape[1]
    tiles = f_send.shape[3]

    loads = [
        pltpu.make_async_copy(src, dst, load_sems.at[i])
        for i, (src, dst) in enumerate((
            (table_hbm, table), (warm_hbm, warm), (analysis_hbm, analysis),
            (thermal_hbm, thermal), (operator_hbm, operator), (order_hbm, order),
        ))
    ]
    for load in loads:
        load.start()

    barrier = pltpu.get_barrier_semaphore()

    def plane(dy, da, db, dc):
        return {
            "y": lax.rem(y + dy, Y), "a": lax.rem(a + da, A),
            "b": lax.rem(b + db, B), "c": lax.rem(c + dc, C),
        }

    columns = [(0, da, db, dc) for da in range(A) for db in range(B) for dc in range(C)][1:]
    rows = [(dy, 0, 0, 0) for dy in range(1, Y)]
    columns.sort(key=lambda step: -min(A * step[2] + step[1], A * B - A * step[2] - step[1]))
    rows.sort(key=lambda step: -min(step[0], Y - step[0]))
    for step in columns + rows:
        pl.semaphore_signal(barrier, inc=1, device_id=plane(*step), device_id_type=MESH)
    for d in range(1, X):
        pl.semaphore_signal(
            barrier, inc=1, device_id={"x": lax.rem(x + d, X)}, device_id_type=MESH
        )

    loads[0].wait()
    rows32[...] = table[...].astype(f32).reshape(bands * own_degrees, M)
    for half in range(2):
        wide = jnp.concatenate(
            [
                rows32[pl.ds(l, bands, stride=own_degrees), :].T
                for l in range(half * own_degrees // 2, (half + 1) * own_degrees // 2)
            ],
            axis=1,
        )
        for tile in range(tiles):
            turned32[tile, pl.ds(half, M, stride=2), :] = wide[:, tile * 128 : (tile + 1) * 128]
    for tile in range(tiles):
        p_send[:, :, :, tile] = turned32[tile].reshape(B, C, K, 2, 128).astype(bf16)

    pl.semaphore_wait(barrier, len(columns) + len(rows) + X - 1)
    for step in rows:
        pl.semaphore_signal(plane_sem, inc=1, device_id=plane(*step), device_id_type=MESH)

    def pair(own, both, sems):
        for other in range(1, C):
            core = lax.rem(c + other, C)
            pltpu.make_async_remote_copy(
                src_ref=own.at[:, core], dst_ref=both.at[:, :, c],
                send_sem=sems.at[0], recv_sem=sems.at[1],
                device_id={"c": core}, device_id_type=MESH,
            ).start()
        pltpu.make_async_copy(own.at[:, c], both.at[:, :, c], sems.at[1]).start()

    pair(p_send, p_pair, p_pair_sems)

    loads[1].wait()
    loads[2].wait()
    fourier = lax.dot_general(
        analysis[...], warm[...].reshape(own_levels * bands, longitudes), NT,
        preferred_element_type=f32,
    )
    for tile in range(tiles):
        f_send[:, :, :, tile] = (
            fourier[:, tile * 128 : (tile + 1) * 128].reshape(B, C, K, 2, 128).astype(bf16)
        )

    pair(f_send, f_pair, f_pair_sems)
    pl.semaphore_wait(plane_sem, len(rows))

    def f_copy(target_b, target_k, chunk):
        return pltpu.make_async_remote_copy(
            src_ref=f_pair.at[target_b, target_k], dst_ref=f_all.at[x, b, k],
            send_sem=f_send_sem, recv_sem=f_sems.at[chunk],
            device_id={"y": target_k // A, "a": lax.rem(target_k, A), "b": target_b},
            device_id_type=MESH,
        )

    def p_copy(target_b, target_k, chunk):
        return pltpu.make_async_remote_copy(
            src_ref=p_pair.at[target_b, target_k], dst_ref=p_recv.at[b, k],
            send_sem=p_sems.at[0], recv_sem=p_sems.at[1],
            device_id={"y": target_k // A, "a": lax.rem(target_k, A), "b": target_b},
            device_id_type=MESH,
        )

    chunks = sorted(range(B), key=lambda step: min(step, B - step))

    def place(sign, chunk):
        return lax.rem(b + sign * chunks[chunk] + B, B)

    def send_chunk(copy, chunk):
        target_b = place(1, chunk)

        def send(i, carry):
            copy(target_b, lax.rem(k + i, K), chunk).start()
            return carry

        lax.fori_loop(1 if chunk == 0 else 0, K, send, 0)

    pltpu.make_async_copy(f_pair, f_pair, f_pair_sems.at[1]).wait()
    pltpu.make_async_copy(f_pair.at[b, k], f_all.at[x, b, k], f_sems.at[0]).start()
    for chunk in range(B):
        send_chunk(f_copy, chunk)
    pltpu.make_async_copy(p_pair, p_pair, p_pair_sems.at[1]).wait()
    pltpu.make_async_copy(p_pair.at[b, k], p_recv.at[b, k], p_sems.at[1]).start()
    for chunk in range(B):
        send_chunk(p_copy, chunk)

    loads[3].wait()
    loads[4].wait()
    for l in range(own_degrees):
        high, low = split(operator[l])
        operator16[l] = high
        t_high, t_low = split(
            jnp.concatenate([thermal[l, :, half, :] for half in range(2)], axis=0)
        )
        own_part[l] = (
            lax.dot_general(t_high, high, NT, preferred_element_type=f32)
            + lax.dot_general(t_low, high, NT, preferred_element_type=f32)
            + lax.dot_general(t_high, low, NT, preferred_element_type=f32)
        )
    loads[5].wait()

    right, left = lax.rem(x + 1, X), lax.rem(x + X - 1, X)
    far = lax.rem(x + 2, X)

    def block(source, chunk):
        return f_all.at[source, place(-1, chunk)]

    def pass_on(source, chunk, target, sem):
        pltpu.make_async_remote_copy(
            src_ref=block(source, chunk), dst_ref=block(source, chunk),
            send_sem=x_send_sem, recv_sem=sem,
            device_id={"x": target}, device_id_type=MESH,
        ).start()

    def arrived(source, chunk, sem):
        pltpu.make_async_copy(block(source, chunk), block(source, chunk), sem).wait()

    for chunk in range(B):
        arrived(x, chunk, f_sems.at[chunk])
        pass_on(x, chunk, right, x_recv_sems.at[0, chunk])
        pass_on(x, chunk, left, x_recv_sems.at[1, chunk])
        pass_on(x, chunk, far, far_sem)

    def spread(buffer, core, parts):
        wide = jnp.concatenate(
            [buffer[:, core, tile].reshape(2 * K, 128) for tile in range(tiles)], axis=1
        )
        return jnp.concatenate(
            [wide[:, part * bands : (part + 1) * bands] for part in range(parts)], axis=0
        )

    width = K * 2 * own_levels
    rows = K * own_degrees

    def spectrum(source):
        total = jnp.zeros((rows, width), f32)
        for band in range(B * C):
            total += lax.dot_general(
                p_rows[band], spread(f_all.at[source, band // C], band % C, own_levels), NT,
                preferred_element_type=f32,
            )
        for l in range(own_degrees // 2):
            total32[pl.ds(l, 2 * K, stride=own_degrees // 2), :] = total[
                l * 2 * K : (l + 1) * 2 * K
            ]
        s_send[source] = total32[...].reshape(K, own_degrees, width).astype(bf16)

        def send(i, carry):
            target = lax.rem(k + i, K)
            pltpu.make_async_remote_copy(
                src_ref=s_send.at[source, target], dst_ref=s_recv.at[source, k],
                send_sem=s_sems.at[0], recv_sem=s_sems.at[1 + source],
                device_id={"y": target // A, "a": lax.rem(target, A)}, device_id_type=MESH,
            ).start()
            return carry

        pltpu.make_async_copy(s_send.at[source, k], s_recv.at[source, k], s_sems.at[1 + source]).start()
        lax.fori_loop(1, K, send, 0)

    pltpu.make_async_copy(p_recv, p_recv, p_sems.at[1]).wait()
    for band in range(B * C):
        p_rows[band] = spread(p_recv.at[band // C], band % C, own_degrees // 2)
    spectrum(x)
    for chunk in range(B):
        arrived(left, chunk, x_recv_sems.at[0, chunk])
    spectrum(left)
    for chunk in range(B):
        arrived(right, chunk, x_recv_sems.at[1, chunk])
    spectrum(right)
    pltpu.make_async_copy(f_all.at[far], f_all.at[far], far_sem).wait()
    spectrum(far)

    half = X * K * own_levels
    ordered = jnp.zeros((rows, 2 * half), f32)
    for source in (x, left, right, far):
        landed = s_recv.at[source]
        pltpu.make_async_copy(landed, landed, s_sems.at[1 + source]).wait()
        ordered += jnp.dot(
            s_recv[source].reshape(rows, width),
            order[pl.ds(pl.multiple_of(source * width, width), width), :],
            preferred_element_type=f32,
        )
    wide = ordered32.shape[1]
    pieces = 2 * half // wide
    for piece in range(pieces):
        ordered32[piece * rows : (piece + 1) * rows] = ordered[:, piece * wide : (piece + 1) * wide]
    for l in range(own_degrees):
        parts = [
            ordered32[pl.ds(piece * rows + l, K, stride=own_degrees), :] for piece in range(pieces)
        ]
        forced = jnp.concatenate(
            [
                jnp.concatenate(parts[: pieces // 2], axis=1),
                jnp.concatenate(parts[pieces // 2 :], axis=1),
            ],
            axis=0,
        )
        out_ref[l] = own_part[l] + lax.dot_general(
            forced.astype(bf16), operator16[l], NT, preferred_element_type=f32
        )

    for _ in range(X - 1):
        pltpu.make_async_copy(f_all.at[x], f_all.at[x], x_send_sem).wait()
    for both, sem in ((f_pair, f_send_sem), (p_pair, p_sems.at[0])):
        sent = both.at[:, pl.ds(0, K - 1)]
        pltpu.make_async_copy(sent, sent, sem).wait()
        sent = both.at[pl.ds(0, B - 1), K - 1]
        pltpu.make_async_copy(sent, sent, sem).wait()
    for own, sems in ((f_send, f_pair_sems), (p_send, p_pair_sems)):
        sent = own.at[:, pl.ds(0, C - 1)]
        pltpu.make_async_copy(sent, sent, sems.at[0]).wait()
    sent = s_send.at[:, pl.ds(0, K - 1)]
    pltpu.make_async_copy(sent, sent, s_sems.at[0]).wait()


def shards(sizes, warming, table, thermal, operator):
    X, Y, A, B, C = sizes
    K = Y * A
    M = table.shape[0]
    own_levels, bands, longitudes = warming.shape
    own_degrees = table.shape[2]
    degrees = own_degrees * X * K
    levels = thermal.shape[3]
    lanes = 128
    tiles = own_levels * bands // lanes
    vmem = pltpu.VMEM
    dma = pltpu.SemaphoreType.DMA
    table = jnp.transpose(table, (1, 2, 0))
    analysis = analysis_rows(M, degrees // M, longitudes)
    order = level_order(X, K, own_levels)
    operands = (warming, table, thermal, operator, analysis, order)
    result = pl.pallas_call(
        functools.partial(kernel, sizes),
        out_shape=jax.ShapeDtypeStruct((own_degrees, 2 * K, levels), f32),
        in_specs=[pl.BlockSpec(memory_space=pl.ANY)] * 6,
        out_specs=pl.BlockSpec(memory_space=pltpu.VMEM),
        scratch_shapes=[
            vmem(warming.shape, bf16),
            vmem(table.shape, bf16),
            vmem(thermal.shape, f32),
            vmem(operator.shape, f32),
            vmem(analysis.shape, bf16),
            vmem(order.shape, bf16),
            vmem((bands * own_degrees, M), f32),
            vmem((tiles, 2 * M, lanes), f32),
            vmem((K * own_degrees, 2 * levels // X), f32),
            vmem((B * C, K * own_degrees, bands), bf16),
            vmem((B, C, K, tiles, 2, lanes), bf16),
            vmem((B, K, C, tiles, 2, lanes), bf16),
            vmem((X, B, K, C, tiles, 2, lanes), bf16),
            vmem((B, C, K, tiles, 2, lanes), bf16),
            vmem((B, K, C, tiles, 2, lanes), bf16),
            vmem((B, K, C, tiles, 2, lanes), bf16),
            vmem((X, K, own_degrees, 2 * levels // X), bf16),
            vmem((X, K, own_degrees, 2 * levels // X), bf16),
            vmem(operator.shape, bf16),
            vmem((own_degrees, 2 * K, levels), f32),
            vmem((2 * levels // min(lanes, levels) * K * own_degrees, min(lanes, levels)), f32),
            dma((6,)), dma((2,)), dma((2,)), dma((2,)), dma, dma((B,)), dma, dma((2, B)), dma, dma((1 + X,)),
            pltpu.SemaphoreType.REGULAR,
        ],
        compiler_params=pltpu.CompilerParams(
            collective_id=0, has_side_effects=True, vmem_limit_bytes=40 * 2**20
        ),
        cost_estimate=pl.CostEstimate(flops=10**9, bytes_accessed=10**7, transcendentals=0),
    )(*(pltpu.with_memory_space_constraint(v, pltpu.HBM) for v in operands))
    return jnp.transpose(result.reshape(own_degrees, 2, K, levels), (0, 2, 1, 3))


def build(mesh, sizes):
    finer = Mesh(mesh.devices.reshape(sizes), ("x", "y", "a", "b", "c"))
    shell, lat = ("x", "y", "a"), ("b", "c")
    in_specs = (
        P(shell, lat, None),
        P(None, lat, shell),
        P(shell, lat, None, None),
        P(shell, None, None),
    )
    return jax.shard_map(
        functools.partial(shards, sizes), mesh=finer, in_specs=in_specs,
        out_specs=P(shell, lat, None, None), check_vma=False,
    )


def solution(mesh):
    return build(mesh, (4, 8, 2, 4, 2))
```
